32 devices in a mesh: groups: 2 (over x), dp: 16 (over z, y, core).
Axes of the slice: x: 2, y: 2, z: 4, core: 2. Of those that a mesh axis runs over, the one named last changes fastest.
Arguments:
- features: bfloat16 [16384, 4096], P(('groups', 'dp')), parts along dimension 0, may hold values from -6 to 6
- upstream: bfloat16 [16384, 512], P(('groups', 'dp')), parts along dimension 0, may hold values from -0.29882812 to 0.29882812
- frozen_value: bfloat16 [4096, 512], replicated, may hold values from -0.25 to 0.25
- adapter_down: bfloat16 [24, 32, 4096], P('groups'), parts along dimension 0, may hold values from -0.09375 to 0.09375
- adapter_up: bfloat16 [24, 32, 512], P('groups'), parts along dimension 0, may hold values from -0.25 to 0.25
- block_adapter: int32 [128, 1], P(('groups', 'dp')), parts along dimension 0, may hold values from 0 to 11
- block_count: int32 [128], P(('groups', 'dp')), parts along dimension 0, may hold values from 1 to 128, as said below
Outputs:
- input_grad: bfloat16 [16384, 4096], P(('groups', 'dp')), parts along dimension 0
- grad_down: float32 [24, 32, 4096], P('groups', None, 'dp'), parts along dimension 0
- grad_up: float32 [24, 32, 512], P('groups', None, 'dp'), parts along dimension 0
The draws below stay inside these ranges and needn't reach their ends.
There are 2 independent parts, one for each index of `groups`. The reference program is written for one: setup_inputs(seed, part) draws one part's arguments, and reference() takes and returns one part's arrays. A program takes and returns all parts, laid end to end along the dimension named above; an argument that names none is the same for every part. Nothing has to cross between parts.
Inputs may be any that keep to these rules, and one draw needn't show every extreme that they name: `block_adapter`: every adapter of 0 to 11 owns some block. Rows 0 to block_count - 1 of a block are live, the rest padding; some block is full and some has one live row.
All inputs are finite; a program needn't handle non-finite values.
Results may differ from the reference program's by a relative error of at most 0.0029.
Values may be sent and summed in bfloat16 or wider, within the bound.
A program may use at most 192 MiB of HBM per device.

```python
import jax
import jax.numpy as jnp
from jax import lax

D = 4096
O = 512
R = 32
BLOCK = 128
ADAPTERS = 12
BLOCKS_ALL = 64
TOKENS = 8192


def draw_block_count(key, part):
    key = jax.random.fold_in(key, 11)
    counts = jax.random.randint(key, (BLOCKS_ALL,), 1, BLOCK + 1)
    counts = counts.at[0].set(BLOCK)
    return counts.at[BLOCKS_ALL - 1].set(1).astype(jnp.int32)


def levels(stream_key, shape, shards, low, top_value):
    gain = 1.0
    for axis_at, blocks in shards:
        heights = jax.random.uniform(jax.random.fold_in(jax.random.fold_in(stream_key, 6), axis_at), (blocks,), jnp.float32, low / len(shards), top_value / len(shards))
        gain = gain * jnp.repeat(jnp.exp(heights), shape[axis_at] // blocks).reshape((-1,) + (1,) * (len(shape) - 1 - axis_at))
    return gain


def choose_distinct(own_key, rows, number_of, top, lift):
    ranking = jax.random.permutation(jax.random.fold_in(own_key, 1), number_of)
    boost = ranking
    for power in range(3):
        boost = boost * boost // number_of
    boost = boost * lift // number_of
    chance = jax.random.randint(jax.random.fold_in(own_key, 2), (rows, number_of), 0, 4096) + boost
    sure = jax.random.permutation(jax.random.fold_in(own_key, 3), rows)[jnp.arange(number_of) % rows]
    chance = jnp.where(jnp.arange(rows)[:, None] == sure[None, :], 1 << 14, chance)
    priority = chance * number_of + jnp.arange(number_of)
    return lax.top_k(priority.astype(jnp.int32), top)[1].astype(jnp.int32)


def centred(key, extent, scale, limit, shards=(), kind=jnp.bfloat16):
    drawn = jax.random.normal(key, extent, jnp.float32) * scale
    if len(shards) > 0:
        drawn = levels(key, extent, shards, -0.22, 0.18) * drawn
    return jnp.clip(drawn, min=-limit, max=limit).astype(kind)


def setup_inputs(seed: int = 0, part: int = 0) -> dict:
    streams_of = jax.random.split(jax.random.key(seed), 8)
    part_splits = jax.random.split(jax.random.fold_in(streams_of[7], part), 8)
    return {
        "features": centred(part_splits[0], (TOKENS, D), 1.0, 6.0, ((0, 16),)),
        "upstream": centred(part_splits[1], (TOKENS, O), 0.05, 0.29882812, ((0, 16),)),
        "frozen_value": centred(streams_of[2], (D, O), O ** -0.5, 0.25),
        "adapter_down": centred(part_splits[3], (ADAPTERS, R, D), D ** -0.5, 0.09375),
        "adapter_up": centred(part_splits[4], (ADAPTERS, R, O), O ** -0.5, 0.25),
        "block_adapter": choose_distinct(part_splits[5], BLOCKS_ALL, ADAPTERS, 1, 1365),
        "block_count": draw_block_count(jax.random.fold_in(jax.random.fold_in(streams_of[7], part), 71), part),
    }


def reference(features, upstream, frozen_value, adapter_down, adapter_up, block_adapter, block_count):
    nblk = block_count.shape[0]
    rows = features.shape[0] // nblk
    ids = block_adapter[:, 0].astype(jnp.int32)
    xblk = features.reshape(nblk, rows, D).astype(jnp.float32)
    yblk = upstream.reshape(nblk, rows, O).astype(jnp.float32)
    down_sel = adapter_down[ids].astype(jnp.float32)
    up_sel = adapter_up[ids].astype(jnp.float32)
    position = lax.broadcasted_iota(jnp.int32, (nblk, rows), 1)
    live = (position < block_count[:, None]).astype(jnp.float32)[:, None, :]
    low_raw = jnp.einsum('brd,bjd->brj', down_sel, xblk, precision=lax.Precision.HIGHEST)
    low = lax.optimization_barrier(low_raw.astype(jnp.bfloat16)).astype(jnp.float32) * live
    back_raw = jnp.einsum('bro,bjo->brj', up_sel, yblk, precision=lax.Precision.HIGHEST)
    back = lax.optimization_barrier(back_raw.astype(jnp.bfloat16)).astype(jnp.float32) * live
    frozen_term = jnp.einsum('bjo,do->bjd', yblk, frozen_value.astype(jnp.float32), precision=lax.Precision.HIGHEST)
    adapter_term = jnp.einsum('brj,brd->bjd', back, down_sel, precision=lax.Precision.HIGHEST)
    input_grad = (live[:, 0, :, None] * (frozen_term + 2.0 * adapter_term)).reshape(nblk * rows, D).astype(jnp.bfloat16)
    part_down = jnp.einsum('brj,bjd->brd', back, xblk, precision=lax.Precision.HIGHEST)
    part_up = jnp.einsum('brj,bjo->bro', low, yblk, precision=lax.Precision.HIGHEST)
    onehot = (ids[:, None] == jnp.arange(ADAPTERS, dtype=jnp.int32)[None, :]).astype(jnp.float32)
    grad_down = 2.0 * jnp.einsum('ba,brd->ard', onehot, part_down, precision=lax.Precision.HIGHEST)
    grad_up = 2.0 * jnp.einsum('ba,bro->aro', onehot, part_up, precision=lax.Precision.HIGHEST)
    return (input_grad, grad_down, grad_up)
```

```python
import functools

import jax
import jax.numpy as jnp
from jax import lax
from jax.experimental import pallas as pl
from jax.experimental.pallas import tpu as pltpu
from jax.sharding import PartitionSpec as P

MESH = pl.DeviceIdType.MESH
BF, F32, I32 = jnp.bfloat16, jnp.float32, jnp.int32
INNER = 4
TILE = 512


def dot_nt(a, b):
    return lax.dot_general(a, b, (((1,), (1,)), ((), ())), preferred_element_type=F32)


def dot_nn(a, b):
    return jnp.dot(a, b, preferred_element_type=F32)


def iota(shape, dim):
    return lax.broadcasted_iota(I32, shape, dim)


def chunk_order(outer):
    rows = []
    for z in range(outer):
        row = []
        for t in range(outer - 1):
            if t >= z:
                row.append(z + outer - 1 - t)
            if t >= outer - 1 - z:
                row.append(t - (outer - 1 - z))
        rows.append(row + [z])
    return rows


def kernel(
    dims,
    ids_ref,
    cnt_ref,
    x_hbm,
    y_hbm,
    fz_hbm,
    dn_hbm,
    up_hbm,
    gin_hbm,
    gdn_ref,
    gup_ref,
    x_v,
    y_v,
    fz_v,
    dn_v,
    up_v,
    dsel,
    ylive,
    back2,
    o_v,
    idm,
    idr,
    msg,
    rmsg,
    umsg,
    rumsg,
    e_down,
    e_up,
    acc,
    uacc,
    ls,
    lr,
    lus,
    lur,
    ld_sem,
    x_sem,
    o_sem,
    id_ss,
    id_rs,
    m_ss,
    m_rs,
    u_ss,
    u_rs,
    l_ss,
    l_rs,
    lu_ss,
    lu_rs,
):
    nblk, rows, rank, tenants, outer, w, oc = dims
    tokens, width = x_v.shape
    outs = y_v.shape[1]
    br = nblk * rank
    slab = INNER * w
    me = lax.axis_index("dp")
    z = me // INNER
    mi = me % INNER
    group = lax.axis_index("groups")

    def dev(d):
        return (group, d)

    loads = [
        pltpu.make_async_copy(y_hbm, y_v, ld_sem.at[0]),
        pltpu.make_async_copy(up_hbm, up_v, ld_sem.at[1]),
        pltpu.make_async_copy(dn_hbm, dn_v, ld_sem.at[2]),
        pltpu.make_async_copy(fz_hbm, fz_v, ld_sem.at[3]),
    ]
    loads[0].start()
    loads[1].start()
    table = chunk_order(outer)
    order = []
    for k in range(outer):
        zk = jnp.int32(0)
        for place in range(outer):
            zk = jnp.where(z == place, table[place][k], zk)
        order.append(zk)

    def slab_of(zc):
        return pl.ds(pl.multiple_of(zc * slab, slab), slab)

    def x_load(zc):
        return pltpu.make_async_copy(x_hbm.at[:, slab_of(zc)], x_v.at[:, slab_of(zc)], x_sem.at[zc])

    for k in range(outer):
        x_load(order[k]).start()
    loads[2].start()
    loads[3].start()

    barrier = pltpu.get_barrier_semaphore()
    for k in range(1, INNER):
        pl.semaphore_signal(barrier, inc=1, device_id=dev(z * INNER + (mi + k) % INNER), device_id_type=MESH)

    @pl.when(z > 0)
    def _():
        pl.semaphore_signal(barrier, inc=1, device_id=dev(me - INNER), device_id_type=MESH)

    @pl.when(z < outer - 1)
    def _():
        pl.semaphore_signal(barrier, inc=1, device_id=dev(me + INNER), device_id_type=MESH)

    lanes = idm.shape[1]
    lane = iota((16, lanes), 1)
    half = iota((16, lanes), 0) < 8
    by_rank = jnp.zeros((16, lanes), F32)
    by_col = jnp.zeros((16, lanes), F32)
    row_id = jnp.zeros((br, 1), I32)
    row_cnt = jnp.zeros((br, 1), I32)
    lane_cnt = jnp.zeros((1, br), I32)
    tok_cnt = jnp.zeros((tokens, 1), I32)
    for b in range(nblk):
        a_b = ids_ref[b, 0]
        c_b = cnt_ref[b]
        by_rank = jnp.where(lane // rank == b, a_b.astype(F32), by_rank)
        by_col = jnp.where(lane // oc == b, a_b.astype(F32), by_col)
        row_id = jnp.where(iota((br, 1), 0) // rank == b, a_b, row_id)
        row_cnt = jnp.where(iota((br, 1), 0) // rank == b, c_b, row_cnt)
        lane_cnt = jnp.where(iota((1, br), 1) // rank == b, c_b, lane_cnt)
        tok_cnt = jnp.where(iota((tokens, 1), 0) // rows == b, c_b, tok_cnt)
    idm[...] = jnp.where(half, by_rank, by_col).astype(BF)
    idr[mi] = idm[...]

    pick_shape = (br, tenants * rank)
    pick = (
        jnp.where(
            (iota(pick_shape, 1) // rank == row_id)
            & (iota(pick_shape, 1) % rank == iota(pick_shape, 0) % rank),
            1.0,
            0.0,
        )
    ).astype(BF)
    shape_t = (br, tokens)
    mask_t = (iota(shape_t, 0) // rank == iota(shape_t, 1) // rows) & (iota(shape_t, 1) % rows < row_cnt)
    shape_n = (tokens, br)
    mask_n = (iota(shape_n, 1) // rank == iota(shape_n, 0) // rows) & (iota(shape_n, 0) % rows < lane_cnt)

    loads[0].wait()
    loads[1].wait()
    up_sel = dot_nn(pick, up_v[...]).astype(BF)
    back_t = jnp.where(mask_t, dot_nt(up_sel, y_v[...]).astype(BF).astype(F32), 0.0).astype(BF)

    def id_copy(k, src_of):
        peer = (mi + k) % INNER
        return pltpu.make_async_remote_copy(
            src_ref=idm,
            dst_ref=idr.at[src_of],
            send_sem=id_ss.at[peer],
            recv_sem=id_rs.at[src_of],
            device_id=dev(z * INNER + peer),
            device_id_type=MESH,
        )

    def m_copy(zc, k, src_of):
        peer = (mi + k) % INNER
        return pltpu.make_async_remote_copy(
            src_ref=msg.at[zc, peer],
            dst_ref=rmsg.at[zc, src_of],
            send_sem=m_ss.at[zc, peer],
            recv_sem=m_rs.at[zc, src_of],
            device_id=dev(z * INNER + peer),
            device_id_type=MESH,
        )

    def u_copy(zc, k, src_of):
        peer = (mi + k) % INNER
        return pltpu.make_async_remote_copy(
            src_ref=umsg.at[zc, peer],
            dst_ref=rumsg.at[zc, src_of],
            send_sem=u_ss.at[zc, peer],
            recv_sem=u_rs.at[zc, src_of],
            device_id=dev(z * INNER + peer),
            device_id_type=MESH,
        )

    def send_chunk(zc):
        x_load(zc).wait()
        part = (2.0 * dot_nn(back_t, x_v[:, slab_of(zc)])).astype(BF)
        for i in range(INNER):
            msg[zc, i] = part[:, i * w : (i + 1) * w]
        for k in range(1, INNER):
            m_copy(zc, k, mi).start()
        rmsg[zc, mi] = msg[zc, mi]

    one = jnp.int32(1)
    pl.semaphore_wait(
        barrier, INNER - 1 + jnp.where(z > 0, one, 0) + jnp.where(z < outer - 1, one, 0)
    )
    for k in range(1, INNER):
        id_copy(k, mi).start()
    send_chunk(order[0])

    loads[2].wait()

    def select_step(j, carry):
        cols = pl.ds(pl.multiple_of(j * TILE, TILE), TILE)
        dsel[:, cols] = dot_nn(pick, dn_v[:, cols]).astype(BF)
        return carry

    lax.fori_loop(0, width // TILE, select_step, 0)
    low_sum = dot_nt(dsel[:, slab_of(order[0])], x_v[:, slab_of(order[0])])
    for k in range(1, outer):
        send_chunk(order[k])
        low_sum = low_sum + dot_nt(dsel[:, slab_of(order[k])], x_v[:, slab_of(order[k])])
    low_t = jnp.where(mask_t, low_sum.astype(BF).astype(F32), 0.0).astype(BF)
    part_up = 2.0 * dot_nn(low_t, y_v[...])
    for zc in range(outer):
        for i in range(INNER):
            at = (zc * INNER + i) * oc
            umsg[zc, i] = jnp.concatenate(
                [part_up[b * rank : (b + 1) * rank, at : at + oc] for b in range(nblk)], axis=1
            ).astype(BF)
    for k in range(outer):
        for j in range(1, INNER):
            u_copy(order[k], j, mi).start()
    for zc in range(outer):
        rumsg[zc, mi] = umsg[zc, mi]

    ylive[...] = jnp.where(
        iota((tokens, 1), 0) % rows < tok_cnt, y_v[...].astype(F32), 0.0
    ).astype(BF)
    back2[...] = jnp.where(
        mask_n, 2.0 * dot_nt(y_v[...], up_sel).astype(BF).astype(F32), 0.0
    ).astype(BF)

    for k in range(1, INNER):
        id_copy(k, (mi + INNER - k) % INNER).wait_recv()
    e_shape = (tenants * rank, br)
    u_shape = (tenants * oc, nblk * oc)
    for i in range(INNER):
        got = idr[i].astype(F32)
        e_down[:, i * br : (i + 1) * br] = jnp.where(
            ((iota(e_shape, 0) // rank).astype(F32) == got[0:1, :br])
            & (iota(e_shape, 0) % rank == iota(e_shape, 1) % rank),
            1.0,
            0.0,
        ).astype(BF)
        e_up[i] = jnp.where(
            ((iota(u_shape, 0) // oc).astype(F32) == got[8:9, : nblk * oc])
            & (iota(u_shape, 0) % oc == iota(u_shape, 1) % oc),
            1.0,
            0.0,
        ).astype(BF)

    tiles = width // TILE
    loads[3].wait()

    def o_copy(j):
        cols = pl.ds(pl.multiple_of(j * TILE, TILE), TILE)
        return pltpu.make_async_copy(o_v.at[:, cols], gin_hbm.at[:, cols], o_sem.at[j])

    def grad_tile(j, carry):
        cols = pl.ds(pl.multiple_of(j * TILE, TILE), TILE)
        o_v[:, cols] = (
            dot_nt(ylive[...], fz_v[cols, :]) + dot_nn(back2[...], dsel[:, cols])
        ).astype(BF)
        o_copy(j).start()
        return carry

    def merged(zc):
        for k in range(1, INNER):
            m_copy(zc, k, (mi + INNER - k) % INNER).wait_recv()
        acc[...] = dot_nn(e_down[...], rmsg[zc].reshape(INNER * br, w))

    def umerged(zc):
        for k in range(1, INNER):
            u_copy(zc, k, (mi + INNER - k) % INNER).wait_recv()
        total = dot_nt(rumsg[zc, 0], e_up[0])
        for i in range(1, INNER):
            total = total + dot_nt(rumsg[zc, i], e_up[i])
        uacc[...] = total

    def line_copy(way, zc, up):
        src, dst = (lus, lur) if up else (ls, lr)
        ss, rs = (lu_ss, lu_rs) if up else (l_ss, l_rs)
        return pltpu.make_async_remote_copy(
            src_ref=src.at[way, zc],
            dst_ref=dst.at[way, zc],
            send_sem=ss.at[way, zc],
            recv_sem=rs.at[way, zc],
            device_id=dev(me + INNER if way == 0 else me - INNER),
            device_id_type=MESH,
        )

    def take(way, zc, up):
        line_copy(way, zc, up).wait_recv()
        if up:
            uacc[...] += lur[way, zc].astype(F32)
        else:
            acc[...] += lr[way, zc].astype(F32)

    def hop(way, zc):
        fed = z > 0 if way == 0 else z < outer - 1
        merged(zc)

        @pl.when(fed)
        def _():
            take(way, zc, False)

        ls[way, zc] = acc[...].astype(BF)
        line_copy(way, zc, False).start()
        umerged(zc)

        @pl.when(fed)
        def _():
            take(way, zc, True)

        lus[way, zc] = uacc[...].astype(BF)
        line_copy(way, zc, True).start()

    first = (2 * tiles) // (outer + 1)
    lax.fori_loop(0, first, grad_tile, 0)

    def line_step(t, carry):
        @pl.when(t >= z)
        def _():
            hop(0, z + outer - 1 - t)

        @pl.when(t >= outer - 1 - z)
        def _():
            hop(1, t - (outer - 1 - z))

        lo = first + (t * (tiles - first)) // (outer - 1)
        hi = first + ((t + 1) * (tiles - first)) // (outer - 1)
        lax.fori_loop(lo, hi, grad_tile, 0)
        return carry

    lax.fori_loop(0, outer - 1, line_step, 0)

    merged(z)
    umerged(z)

    @pl.when(z > 0)
    def _():
        take(0, z, False)
        take(0, z, True)

    @pl.when(z < outer - 1)
    def _():
        take(1, z, False)
        take(1, z, True)

    gdn_ref[...] = acc[...]
    gup_ref[...] = uacc[...]

    for k in range(1, INNER):
        id_copy(k, mi).wait_send()

    def drain(zc, carry):
        for k in range(1, INNER):
            m_copy(zc, k, mi).wait_send()
            u_copy(zc, k, mi).wait_send()

        @pl.when(zc > z)
        def _():
            line_copy(0, zc, False).wait_send()
            line_copy(0, zc, True).wait_send()

        @pl.when(zc < z)
        def _():
            line_copy(1, zc, False).wait_send()
            line_copy(1, zc, True).wait_send()

        return carry

    lax.fori_loop(0, outer, drain, 0)

    def drain_out(j, carry):
        o_copy(j).wait()
        return carry

    lax.fori_loop(0, tiles, drain_out, 0)


def per_device(
    features, upstream, frozen_value, adapter_down, adapter_up, block_adapter, block_count, *, n
):
    tokens, width = features.shape
    outs = upstream.shape[1]
    tenants, rank = adapter_down.shape[:2]
    nblk = block_count.shape[0]
    rows = tokens // nblk
    outer = n // INNER
    w, oc = width // n, outs // n
    br = nblk * rank
    lanes = max(br, nblk * oc)
    ar = tenants * rank
    dims = (nblk, rows, rank, tenants, outer, w, oc)
    V = pltpu.VMEM
    D = pltpu.SemaphoreType.DMA
    anyspec = pl.BlockSpec(memory_space=pl.ANY)
    smem = pl.BlockSpec(memory_space=pltpu.SMEM)
    vmem = pl.BlockSpec(memory_space=pltpu.VMEM)
    gin, gdn, gup = pl.pallas_call(
        functools.partial(kernel, dims),
        out_shape=(
            jax.ShapeDtypeStruct((tokens, width), BF),
            jax.ShapeDtypeStruct((ar, w), F32),
            jax.ShapeDtypeStruct((rank, tenants * oc), F32),
        ),
        in_specs=[smem, smem] + [anyspec] * 5,
        out_specs=(anyspec, vmem, vmem),
        scratch_shapes=[
            V((tokens, width), BF),
            V((tokens, outs), BF),
            V((width, outs), BF),
            V((ar, width), BF),
            V((ar, outs), BF),
            V((br, width), BF),
            V((tokens, outs), BF),
            V((tokens, br), BF),
            V((tokens, width), BF),
            V((16, lanes), BF),
            V((INNER, 16, lanes), BF),
            V((outer, INNER, br, w), BF),
            V((outer, INNER, br, w), BF),
            V((outer, INNER, rank, nblk * oc), BF),
            V((outer, INNER, rank, nblk * oc), BF),
            V((ar, INNER * br), BF),
            V((INNER, tenants * oc, nblk * oc), BF),
            V((ar, w), F32),
            V((rank, tenants * oc), F32),
            V((2, outer, ar, w), BF),
            V((2, outer, ar, w), BF),
            V((2, outer, rank, tenants * oc), BF),
            V((2, outer, rank, tenants * oc), BF),
            D((4,)),
            D((outer,)),
            D((width // TILE,)),
            D((INNER,)),
            D((INNER,)),
            D((outer, INNER)),
            D((outer, INNER)),
            D((outer, INNER)),
            D((outer, INNER)),
            D((2, outer)),
            D((2, outer)),
            D((2, outer)),
            D((2, outer)),
        ],
        compiler_params=pltpu.CompilerParams(
            collective_id=0, has_side_effects=True, vmem_limit_bytes=56 * 1024 * 1024
        ),
        cost_estimate=pl.CostEstimate(
            flops=2 * tokens * width * (outs + 3 * br),
            bytes_accessed=2 * (2 * tokens * width + width * outs + ar * width),
            transcendentals=0,
        ),
    )(
        block_adapter,
        block_count,
        features,
        upstream,
        frozen_value,
        adapter_down.reshape(ar, width),
        adapter_up.reshape(ar, outs),
    )
    grad_up = gup.reshape(rank, tenants, oc).transpose(1, 0, 2)
    return gin, gdn.reshape(tenants, rank, w), grad_up


def solution(mesh):
    return jax.shard_map(
        functools.partial(per_device, n=mesh.shape["dp"]),
        mesh=mesh,
        in_specs=(
            P(("groups", "dp"), None),
            P(("groups", "dp"), None),
            P(),
            P("groups", None, None),
            P("groups", None, None),
            P(("groups", "dp"), None),
            P(("groups", "dp")),
        ),
        out_specs=(P(("groups", "dp"), None), P("groups", None, "dp"), P("groups", None, "dp")),
        check_vma=False,
    )
```

```python
import functools

import jax
import jax.numpy as jnp
from jax import lax
from jax.experimental import pallas as pl
from jax.experimental.pallas import tpu as pltpu
from jax.sharding import PartitionSpec as P

MESH = pl.DeviceIdType.MESH
BF, F32, I32 = jnp.bfloat16, jnp.float32, jnp.int32
INNER = 4
TILE = 512


def dot_nt(a, b):
    return lax.dot_general(a, b, (((1,), (1,)), ((), ())), preferred_element_type=F32)


def dot_nn(a, b):
    return jnp.dot(a, b, preferred_element_type=F32)


def iota(shape, dim):
    return lax.broadcasted_iota(I32, shape, dim)


def chunk_order(outer):
    rows = []
    for z in range(outer):
        row = []
        for t in range(outer - 1):
            if t >= z:
                row.append(z + outer - 1 - t)
            if t >= outer - 1 - z:
                row.append(t - (outer - 1 - z))
        rows.append(row + [z])
    return rows


def kernel(
    dims,
    ids_ref,
    cnt_ref,
    x_hbm,
    y_hbm,
    fz_hbm,
    dn_hbm,
    up_hbm,
    o_v,
    gdn_ref,
    gup_ref,
    x_v,
    y_v,
    fz_v,
    dn_v,
    up_v,
    dsel,
    ylive,
    back2,
    idm,
    idr,
    msg,
    rmsg,
    umsg,
    rumsg,
    e_down,
    e_up,
    acc,
    uacc,
    ls,
    lr,
    lus,
    lur,
    ld_sem,
    x_sem,
    id_ss,
    id_rs,
    m_ss,
    m_rs,
    u_ss,
    u_rs,
    l_ss,
    l_rs,
    lu_ss,
    lu_rs,
):
    nblk, rows, rank, tenants, outer, w, oc = dims
    tokens, width = x_v.shape
    outs = y_v.shape[1]
    br = nblk * rank
    slab = INNER * w
    me = lax.axis_index("dp")
    z = me // INNER
    mi = me % INNER
    group = lax.axis_index("groups")

    def dev(d):
        return (group, d)

    loads = [
        pltpu.make_async_copy(y_hbm, y_v, ld_sem.at[0]),
        pltpu.make_async_copy(up_hbm, up_v, ld_sem.at[1]),
        pltpu.make_async_copy(dn_hbm, dn_v, ld_sem.at[2]),
        pltpu.make_async_copy(fz_hbm, fz_v, ld_sem.at[3]),
    ]
    loads[0].start()
    loads[1].start()
    table = chunk_order(outer)
    order = []
    for k in range(outer):
        zk = jnp.int32(0)
        for place in range(outer):
            zk = jnp.where(z == place, table[place][k], zk)
        order.append(zk)

    def slab_of(zc):
        return pl.ds(pl.multiple_of(zc * slab, slab), slab)

    def x_load(zc):
        return pltpu.make_async_copy(x_hbm.at[:, slab_of(zc)], x_v.at[:, slab_of(zc)], x_sem.at[zc])

    for k in range(outer):
        x_load(order[k]).start()
    loads[2].start()
    loads[3].start()

    barrier = pltpu.get_barrier_semaphore()
    for k in range(1, INNER):
        pl.semaphore_signal(barrier, inc=1, device_id=dev(z * INNER + (mi + k) % INNER), device_id_type=MESH)

    @pl.when(z > 0)
    def _():
        pl.semaphore_signal(barrier, inc=1, device_id=dev(me - INNER), device_id_type=MESH)

    @pl.when(z < outer - 1)
    def _():
        pl.semaphore_signal(barrier, inc=1, device_id=dev(me + INNER), device_id_type=MESH)

    lanes = idm.shape[1]
    lane = iota((16, lanes), 1)
    half = iota((16, lanes), 0) < 8
    by_rank = jnp.zeros((16, lanes), F32)
    by_col = jnp.zeros((16, lanes), F32)
    row_id = jnp.zeros((br, 1), I32)
    row_cnt = jnp.zeros((br, 1), I32)
    lane_cnt = jnp.zeros((1, br), I32)
    tok_cnt = jnp.zeros((tokens, 1), I32)
    for b in range(nblk):
        a_b = ids_ref[b]
        c_b = cnt_ref[b]
        by_rank = jnp.where(lane // rank == b, a_b.astype(F32), by_rank)
        by_col = jnp.where(lane // oc == b, a_b.astype(F32), by_col)
        row_id = jnp.where(iota((br, 1), 0) // rank == b, a_b, row_id)
        row_cnt = jnp.where(iota((br, 1), 0) // rank == b, c_b, row_cnt)
        lane_cnt = jnp.where(iota((1, br), 1) // rank == b, c_b, lane_cnt)
        tok_cnt = jnp.where(iota((tokens, 1), 0) // rows == b, c_b, tok_cnt)
    idm[...] = jnp.where(half, by_rank, by_col).astype(BF)
    idr[mi] = idm[...]

    pick_shape = (br, tenants * rank)
    pick = (
        jnp.where(
            (iota(pick_shape, 1) // rank == row_id)
            & (iota(pick_shape, 1) % rank == iota(pick_shape, 0) % rank),
            1.0,
            0.0,
        )
    ).astype(BF)
    shape_t = (br, tokens)
    mask_t = (iota(shape_t, 0) // rank == iota(shape_t, 1) // rows) & (iota(shape_t, 1) % rows < row_cnt)
    shape_n = (tokens, br)
    mask_n = (iota(shape_n, 1) // rank == iota(shape_n, 0) // rows) & (iota(shape_n, 0) % rows < lane_cnt)

    loads[0].wait()
    loads[1].wait()
    up_sel = dot_nn(pick, up_v[...]).astype(BF)
    back_t = jnp.where(mask_t, dot_nt(up_sel, y_v[...]).astype(BF).astype(F32), 0.0).astype(BF)

    def id_copy(k, src_of):
        peer = (mi + k) % INNER
        return pltpu.make_async_remote_copy(
            src_ref=idm,
            dst_ref=idr.at[src_of],
            send_sem=id_ss.at[peer],
            recv_sem=id_rs.at[src_of],
            device_id=dev(z * INNER + peer),
            device_id_type=MESH,
        )

    def m_copy(zc, k, src_of):
        peer = (mi + k) % INNER
        return pltpu.make_async_remote_copy(
            src_ref=msg.at[zc, peer],
            dst_ref=rmsg.at[zc, src_of],
            send_sem=m_ss.at[zc, peer],
            recv_sem=m_rs.at[zc, src_of],
            device_id=dev(z * INNER + peer),
            device_id_type=MESH,
        )

    def u_copy(zc, k, src_of):
        peer = (mi + k) % INNER
        return pltpu.make_async_remote_copy(
            src_ref=umsg.at[zc, peer],
            dst_ref=rumsg.at[zc, src_of],
            send_sem=u_ss.at[zc, peer],
            recv_sem=u_rs.at[zc, src_of],
            device_id=dev(z * INNER + peer),
            device_id_type=MESH,
        )

    def send_chunk(zc):
        part = (2.0 * dot_nn(back_t, x_v[:, slab_of(zc)])).astype(BF)
        for i in range(INNER):
            msg[zc, i] = part[:, i * w : (i + 1) * w]
        for k in range(1, INNER):
            m_copy(zc, k, mi).start()
        rmsg[zc, mi] = msg[zc, mi]

    one = jnp.int32(1)
    pl.semaphore_wait(
        barrier, INNER - 1 + jnp.where(z > 0, one, 0) + jnp.where(z < outer - 1, one, 0)
    )
    for k in range(1, INNER):
        id_copy(k, mi).start()
    x_load(order[0]).wait()
    send_chunk(order[0])

    loads[2].wait()

    def select_step(j, carry):
        cols = pl.ds(pl.multiple_of(j * TILE, TILE), TILE)
        dsel[:, cols] = dot_nn(pick, dn_v[:, cols]).astype(BF)
        return carry

    lax.fori_loop(0, width // TILE, select_step, 0)
    for k in range(1, outer):
        x_load(order[k]).wait()
    low = dot_nt(x_v[...], dsel[...]).astype(BF).astype(F32)
    low_t = jnp.where(mask_t, low.T, 0.0).astype(BF)
    part_up = 2.0 * dot_nn(low_t, y_v[...])
    for zc in range(outer):
        for i in range(INNER):
            at = (zc * INNER + i) * oc
            umsg[zc, i] = jnp.concatenate(
                [part_up[b * rank : (b + 1) * rank, at : at + oc] for b in range(nblk)], axis=1
            ).astype(BF)
    for k in range(outer):
        for j in range(1, INNER):
            u_copy(order[k], j, mi).start()
    send_chunk(order[1])
    for zc in range(outer):
        rumsg[zc, mi] = umsg[zc, mi]

    ylive[...] = jnp.where(
        iota((tokens, 1), 0) % rows < tok_cnt, y_v[...].astype(F32), 0.0
    ).astype(BF)
    back2[...] = jnp.where(
        mask_n, 2.0 * dot_nt(y_v[...], up_sel).astype(BF).astype(F32), 0.0
    ).astype(BF)

    for k in range(1, INNER):
        id_copy(k, (mi + INNER - k) % INNER).wait_recv()
    e_shape = (tenants * rank, br)
    u_shape = (tenants * oc, nblk * oc)
    for i in range(INNER):
        got = idr[i].astype(F32)
        e_down[:, i * br : (i + 1) * br] = jnp.where(
            ((iota(e_shape, 0) // rank).astype(F32) == got[0:1, :br])
            & (iota(e_shape, 0) % rank == iota(e_shape, 1) % rank),
            1.0,
            0.0,
        ).astype(BF)
        e_up[i] = jnp.where(
            ((iota(u_shape, 0) // oc).astype(F32) == got[8:9, : nblk * oc])
            & (iota(u_shape, 0) % oc == iota(u_shape, 1) % oc),
            1.0,
            0.0,
        ).astype(BF)

    tiles = width // TILE
    loads[3].wait()

    def grad_tile(j, carry):
        cols = pl.ds(pl.multiple_of(j * TILE, TILE), TILE)
        o_v[:, cols] = (
            dot_nt(ylive[...], fz_v[cols, :]) + dot_nn(back2[...], dsel[:, cols])
        ).astype(BF)
        return carry

    def merged(zc):
        for k in range(1, INNER):
            m_copy(zc, k, (mi + INNER - k) % INNER).wait_recv()
        acc[...] = dot_nn(e_down[...], rmsg[zc].reshape(INNER * br, w))

    def umerged(zc):
        for k in range(1, INNER):
            u_copy(zc, k, (mi + INNER - k) % INNER).wait_recv()
        total = dot_nt(rumsg[zc, 0], e_up[0])
        for i in range(1, INNER):
            total = total + dot_nt(rumsg[zc, i], e_up[i])
        uacc[...] = total

    def line_copy(way, zc, up):
        src, dst = (lus, lur) if up else (ls, lr)
        ss, rs = (lu_ss, lu_rs) if up else (l_ss, l_rs)
        return pltpu.make_async_remote_copy(
            src_ref=src.at[way, zc],
            dst_ref=dst.at[way, zc],
            send_sem=ss.at[way, zc],
            recv_sem=rs.at[way, zc],
            device_id=dev(me + INNER if way == 0 else me - INNER),
            device_id_type=MESH,
        )

    def take(way, zc, up):
        line_copy(way, zc, up).wait_recv()
        if up:
            uacc[...] += lur[way, zc].astype(F32)
        else:
            acc[...] += lr[way, zc].astype(F32)

    def hop(way, zc):
        fed = z > 0 if way == 0 else z < outer - 1
        merged(zc)

        @pl.when(fed)
        def _():
            take(way, zc, False)

        ls[way, zc] = acc[...].astype(BF)
        line_copy(way, zc, False).start()
        umerged(zc)

        @pl.when(fed)
        def _():
            take(way, zc, True)

        lus[way, zc] = uacc[...].astype(BF)
        line_copy(way, zc, True).start()

    first = 0
    lax.fori_loop(0, first, grad_tile, 0)

    def line_step(t, carry):
        @pl.when(t >= z)
        def _():
            hop(0, z + outer - 1 - t)

        @pl.when(t >= outer - 1 - z)
        def _():
            hop(1, t - (outer - 1 - z))

        lo = first + (t * (tiles - first)) // (outer - 1)
        hi = first + ((t + 1) * (tiles - first)) // (outer - 1)
        lax.fori_loop(lo, hi, grad_tile, 0)
        return carry

    for t in range(outer - 1):
        line_step(t, 0)
        if t + 2 < outer:
            send_chunk(order[t + 2])

    merged(z)
    umerged(z)

    @pl.when(z > 0)
    def _():
        take(0, z, False)
        take(0, z, True)

    @pl.when(z < outer - 1)
    def _():
        take(1, z, False)
        take(1, z, True)

    for a in range(tenants):
        gdn_ref[a] = acc[a * rank : (a + 1) * rank, :]
        gup_ref[a] = uacc[:, a * oc : (a + 1) * oc]

    for k in range(1, INNER):
        id_copy(k, mi).wait_send()

    def drain(zc, carry):
        for k in range(1, INNER):
            m_copy(zc, k, mi).wait_send()
            u_copy(zc, k, mi).wait_send()

        @pl.when(zc > z)
        def _():
            line_copy(0, zc, False).wait_send()
            line_copy(0, zc, True).wait_send()

        @pl.when(zc < z)
        def _():
            line_copy(1, zc, False).wait_send()
            line_copy(1, zc, True).wait_send()

        return carry

    lax.fori_loop(0, outer, drain, 0)


def per_device(
    features, upstream, frozen_value, adapter_down, adapter_up, block_adapter, block_count, *, n
):
    tokens, width = features.shape
    outs = upstream.shape[1]
    tenants, rank = adapter_down.shape[:2]
    nblk = block_count.shape[0]
    rows = tokens // nblk
    outer = n // INNER
    w, oc = width // n, outs // n
    br = nblk * rank
    lanes = max(br, nblk * oc)
    ar = tenants * rank
    dims = (nblk, rows, rank, tenants, outer, w, oc)
    V = pltpu.VMEM
    D = pltpu.SemaphoreType.DMA
    anyspec = pl.BlockSpec(memory_space=pl.ANY)
    smem = pl.BlockSpec(memory_space=pltpu.SMEM)
    vmem = pl.BlockSpec(memory_space=pltpu.VMEM)
    gin, gdn, gup = pl.pallas_call(
        functools.partial(kernel, dims),
        out_shape=(
            pltpu.VMEM((tokens, width), BF),
            jax.ShapeDtypeStruct((tenants, rank, w), F32),
            jax.ShapeDtypeStruct((tenants, rank, oc), F32),
        ),
        in_specs=[smem, smem] + [anyspec] * 5,
        out_specs=(vmem, vmem, vmem),
        scratch_shapes=[
            V((tokens, width), BF),
            V((tokens, outs), BF),
            V((width, outs), BF),
            V((ar, width), BF),
            V((ar, outs), BF),
            V((br, width), BF),
            V((tokens, outs), BF),
            V((tokens, br), BF),
            V((16, lanes), BF),
            V((INNER, 16, lanes), BF),
            V((outer, INNER, br, w), BF),
            V((outer, INNER, br, w), BF),
            V((outer, INNER, rank, nblk * oc), BF),
            V((outer, INNER, rank, nblk * oc), BF),
            V((ar, INNER * br), BF),
            V((INNER, tenants * oc, nblk * oc), BF),
            V((ar, w), F32),
            V((rank, tenants * oc), F32),
            V((2, outer, ar, w), BF),
            V((2, outer, ar, w), BF),
            V((2, outer, rank, tenants * oc), BF),
            V((2, outer, rank, tenants * oc), BF),
            D((4,)),
            D((outer,)),
            D((INNER,)),
            D((INNER,)),
            D((outer, INNER)),
            D((outer, INNER)),
            D((outer, INNER)),
            D((outer, INNER)),
            D((2, outer)),
            D((2, outer)),
            D((2, outer)),
            D((2, outer)),
        ],
        compiler_params=pltpu.CompilerParams(
            collective_id=0, has_side_effects=True, vmem_limit_bytes=58 * 1024 * 1024
        ),
        cost_estimate=pl.CostEstimate(
            flops=2 * tokens * width * (outs + 3 * br),
            bytes_accessed=2 * (2 * tokens * width + width * outs + ar * width),
            transcendentals=0,
        ),
    )(
        block_adapter.reshape(nblk),
        block_count,
        features,
        upstream,
        frozen_value,
        adapter_down.reshape(ar, width),
        adapter_up.reshape(ar, outs),
    )
    return gin, gdn, gup


def solution(mesh):
    return jax.shard_map(
        functools.partial(per_device, n=mesh.shape["dp"]),
        mesh=mesh,
        in_specs=(
            P(("groups", "dp"), None),
            P(("groups", "dp"), None),
            P(),
            P("groups", None, None),
            P("groups", None, None),
            P(("groups", "dp"), None),
            P(("groups", "dp")),
        ),
        out_specs=(P(("groups", "dp"), None), P("groups", None, "dp"), P("groups", None, "dp")),
        check_vma=False,
    )
```

```python
import functools

import jax
import jax.numpy as jnp
from jax import lax
from jax.experimental import pallas as pl
from jax.experimental.pallas import tpu as pltpu
from jax.sharding import PartitionSpec as P

MESH = pl.DeviceIdType.MESH
BF, F32, I32 = jnp.bfloat16, jnp.float32, jnp.int32
INNER = 4
TILE = 512


def dot_nt(a, b):
    return lax.dot_general(a, b, (((1,), (1,)), ((), ())), preferred_element_type=F32)


def dot_nn(a, b):
    return jnp.dot(a, b, preferred_element_type=F32)


def iota(shape, dim):
    return lax.broadcasted_iota(I32, shape, dim)


def chunk_order(outer):
    rows = []
    for z in range(outer):
        row = []
        for t in range(outer - 1):
            if t >= z:
                row.append(z + outer - 1 - t)
            if t >= outer - 1 - z:
                row.append(t - (outer - 1 - z))
        rows.append(row + [z])
    return rows


def kernel(
    dims,
    ids_ref,
    cnt_ref,
    x_hbm,
    y_hbm,
    fz_hbm,
    dn_hbm,
    up_hbm,
    o_v,
    gdn_ref,
    gup_ref,
    x_v,
    y_v,
    fz_v,
    dn_v,
    up_v,
    dsel,
    ylive,
    back2,
    idm,
    idr,
    msg,
    rmsg,
    umsg,
    rumsg,
    e_down,
    e_up,
    acc,
    uacc,
    ls,
    lr,
    lus,
    lur,
    ld_sem,
    x_sem,
    id_ss,
    id_rs,
    m_ss,
    m_rs,
    u_ss,
    u_rs,
    l_ss,
    l_rs,
    lu_ss,
    lu_rs,
):
    nblk, rows, rank, tenants, outer, w, oc = dims
    tokens, width = x_v.shape
    outs = y_v.shape[1]
    br = nblk * rank
    slab = INNER * w
    me = lax.axis_index("dp")
    z = me // INNER
    mi = me % INNER
    group = lax.axis_index("groups")

    def dev(d):
        return (group, d)

    loads = [
        pltpu.make_async_copy(y_hbm, y_v, ld_sem.at[0]),
        pltpu.make_async_copy(up_hbm, up_v, ld_sem.at[1]),
        pltpu.make_async_copy(dn_hbm, dn_v, ld_sem.at[2]),
        pltpu.make_async_copy(fz_hbm, fz_v, ld_sem.at[3]),
    ]
    loads[0].start()
    loads[1].start()
    table = chunk_order(outer)
    order = []
    for k in range(outer):
        zk = jnp.int32(0)
        for place in range(outer):
            zk = jnp.where(z == place, table[place][k], zk)
        order.append(zk)

    def slab_of(zc):
        return pl.ds(pl.multiple_of(zc * slab, slab), slab)

    def x_load(zc):
        return pltpu.make_async_copy(x_hbm.at[:, slab_of(zc)], x_v.at[:, slab_of(zc)], x_sem.at[zc])

    for k in range(outer):
        x_load(order[k]).start()
    loads[2].start()
    loads[3].start()

    barrier = pltpu.get_barrier_semaphore()
    for k in range(1, INNER):
        pl.semaphore_signal(barrier, inc=1, device_id=dev(z * INNER + (mi + k) % INNER), device_id_type=MESH)

    @pl.when(z > 0)
    def _():
        pl.semaphore_signal(barrier, inc=1, device_id=dev(me - INNER), device_id_type=MESH)

    @pl.when(z < outer - 1)
    def _():
        pl.semaphore_signal(barrier, inc=1, device_id=dev(me + INNER), device_id_type=MESH)

    lanes = idm.shape[1]
    lane = iota((16, lanes), 1)
    half = iota((16, lanes), 0) < 8
    by_rank = jnp.zeros((16, lanes), F32)
    by_col = jnp.zeros((16, lanes), F32)
    row_id = jnp.zeros((br, 1), I32)
    row_cnt = jnp.zeros((br, 1), I32)
    lane_cnt = jnp.zeros((1, br), I32)
    tok_cnt = jnp.zeros((tokens, 1), I32)
    for b in range(nblk):
        a_b = ids_ref[b]
        c_b = cnt_ref[b]
        by_rank = jnp.where(lane // rank == b, a_b.astype(F32), by_rank)
        by_col = jnp.where(lane // oc == b, a_b.astype(F32), by_col)
        row_id = jnp.where(iota((br, 1), 0) // rank == b, a_b, row_id)
        row_cnt = jnp.where(iota((br, 1), 0) // rank == b, c_b, row_cnt)
        lane_cnt = jnp.where(iota((1, br), 1) // rank == b, c_b, lane_cnt)
        tok_cnt = jnp.where(iota((tokens, 1), 0) // rows == b, c_b, tok_cnt)
    idm[...] = jnp.where(half, by_rank, by_col).astype(BF)
    idr[mi] = idm[...]

    pick_shape = (br, tenants * rank)
    pick = (
        jnp.where(
            (iota(pick_shape, 1) // rank == row_id)
            & (iota(pick_shape, 1) % rank == iota(pick_shape, 0) % rank),
            1.0,
            0.0,
        )
    ).astype(BF)
    shape_t = (br, tokens)
    mask_t = (iota(shape_t, 0) // rank == iota(shape_t, 1) // rows) & (iota(shape_t, 1) % rows < row_cnt)
    shape_n = (tokens, br)
    mask_n = (iota(shape_n, 1) // rank == iota(shape_n, 0) // rows) & (iota(shape_n, 0) % rows < lane_cnt)

    loads[0].wait()
    loads[1].wait()
    up_sel = dot_nn(pick, up_v[...]).astype(BF)
    back_t = jnp.where(mask_t, dot_nt(up_sel, y_v[...]).astype(BF).astype(F32), 0.0).astype(BF)

    def id_copy(k, src_of):
        peer = (mi + k) % INNER
        return pltpu.make_async_remote_copy(
            src_ref=idm,
            dst_ref=idr.at[src_of],
            send_sem=id_ss.at[peer],
            recv_sem=id_rs.at[src_of],
            device_id=dev(z * INNER + peer),
            device_id_type=MESH,
        )

    def m_copy(zc, k, src_of):
        peer = (mi + k) % INNER
        return pltpu.make_async_remote_copy(
            src_ref=msg.at[zc, peer],
            dst_ref=rmsg.at[zc, src_of],
            send_sem=m_ss.at[zc, peer],
            recv_sem=m_rs.at[zc, src_of],
            device_id=dev(z * INNER + peer),
            device_id_type=MESH,
        )

    def u_copy(zc, k, src_of):
        peer = (mi + k) % INNER
        return pltpu.make_async_remote_copy(
            src_ref=umsg.at[zc, peer],
            dst_ref=rumsg.at[zc, src_of],
            send_sem=u_ss.at[zc, peer],
            recv_sem=u_rs.at[zc, src_of],
            device_id=dev(z * INNER + peer),
            device_id_type=MESH,
        )

    def send_chunk(zc):
        part = (2.0 * dot_nn(back_t, x_v[:, slab_of(zc)])).astype(BF)
        for i in range(INNER):
            msg[zc, i] = part[:, i * w : (i + 1) * w]
        for k in range(1, INNER):
            m_copy(zc, k, mi).start()
        rmsg[zc, mi] = msg[zc, mi]

    one = jnp.int32(1)
    pl.semaphore_wait(
        barrier, INNER - 1 + jnp.where(z > 0, one, 0) + jnp.where(z < outer - 1, one, 0)
    )
    for k in range(1, INNER):
        id_copy(k, mi).start()
    x_load(order[0]).wait()
    send_chunk(order[0])

    loads[2].wait()

    def select_step(j, carry):
        cols = pl.ds(pl.multiple_of(j * TILE, TILE), TILE)
        dsel[:, cols] = dot_nn(pick, dn_v[:, cols]).astype(BF)
        return carry

    lax.fori_loop(0, width // TILE, select_step, 0)
    for k in range(1, outer):
        x_load(order[k]).wait()
    low = dot_nt(x_v[...], dsel[...]).astype(BF).astype(F32)
    low_t = jnp.where(mask_t, low.T, 0.0).astype(BF)
    part_up = 2.0 * dot_nn(low_t, y_v[...])
    for zc in range(outer):
        for i in range(INNER):
            at = (zc * INNER + i) * oc
            umsg[zc, i] = jnp.concatenate(
                [part_up[b * rank : (b + 1) * rank, at : at + oc] for b in range(nblk)], axis=1
            ).astype(BF)
    for k in range(outer):
        for j in range(1, INNER):
            u_copy(order[k], j, mi).start()
    send_chunk(order[1])
    for zc in range(outer):
        rumsg[zc, mi] = umsg[zc, mi]

    ylive[...] = jnp.where(
        iota((tokens, 1), 0) % rows < tok_cnt, y_v[...].astype(F32), 0.0
    ).astype(BF)
    back2[...] = jnp.where(
        mask_n, 2.0 * dot_nt(y_v[...], up_sel).astype(BF).astype(F32), 0.0
    ).astype(BF)

    for k in range(1, INNER):
        id_copy(k, (mi + INNER - k) % INNER).wait_recv()
    e_shape = (tenants * rank, br)
    u_shape = (tenants * oc, nblk * oc)
    for i in range(INNER):
        got = idr[i].astype(F32)
        e_down[:, i * br : (i + 1) * br] = jnp.where(
            ((iota(e_shape, 0) // rank).astype(F32) == got[0:1, :br])
            & (iota(e_shape, 0) % rank == iota(e_shape, 1) % rank),
            1.0,
            0.0,
        ).astype(BF)
        e_up[i] = jnp.where(
            ((iota(u_shape, 0) // oc).astype(F32) == got[8:9, : nblk * oc])
            & (iota(u_shape, 0) % oc == iota(u_shape, 1) % oc),
            1.0,
            0.0,
        ).astype(BF)

    tiles = width // TILE
    loads[3].wait()

    def grad_tile(j, carry):
        cols = pl.ds(pl.multiple_of(j * TILE, TILE), TILE)
        o_v[:, cols] = (
            dot_nt(ylive[...], fz_v[cols, :]) + dot_nn(back2[...], dsel[:, cols])
        ).astype(BF)
        return carry

    def merged(zc):
        for k in range(1, INNER):
            m_copy(zc, k, (mi + INNER - k) % INNER).wait_recv()
        acc[...] = dot_nn(e_down[...], rmsg[zc].reshape(INNER * br, w))

    def umerged(zc):
        for k in range(1, INNER):
            u_copy(zc, k, (mi + INNER - k) % INNER).wait_recv()
        total = dot_nt(rumsg[zc, 0], e_up[0])
        for i in range(1, INNER):
            total = total + dot_nt(rumsg[zc, i], e_up[i])
        uacc[...] = total

    def line_copy(way, zc, up):
        src, dst = (lus, lur) if up else (ls, lr)
        ss, rs = (lu_ss, lu_rs) if up else (l_ss, l_rs)
        return pltpu.make_async_remote_copy(
            src_ref=src.at[way, zc],
            dst_ref=dst.at[way, zc],
            send_sem=ss.at[way, zc],
            recv_sem=rs.at[way, zc],
            device_id=dev(me + INNER if way == 0 else me - INNER),
            device_id_type=MESH,
        )

    def take(way, zc, up):
        line_copy(way, zc, up).wait_recv()
        if up:
            uacc[...] += lur[way, zc].astype(F32)
        else:
            acc[...] += lr[way, zc].astype(F32)

    def hop(way, zc):
        fed = z > 0 if way == 0 else z < outer - 1
        merged(zc)

        @pl.when(fed)
        def _():
            take(way, zc, False)

        ls[way, zc] = acc[...].astype(BF)
        line_copy(way, zc, False).start()

    def up_hop(way, zc):
        fed = z > 0 if way == 0 else z < outer - 1
        umerged(zc)

        @pl.when(fed)
        def _():
            take(way, zc, True)

        lus[way, zc] = uacc[...].astype(BF)
        line_copy(way, zc, True).start()

    first = 0
    lax.fori_loop(0, first, grad_tile, 0)

    def line_step(t, carry):
        @pl.when(t >= z)
        def _():
            hop(0, z + outer - 1 - t)

        @pl.when(t >= outer - 1 - z)
        def _():
            hop(1, t - (outer - 1 - z))

        @pl.when(t >= z)
        def _():
            up_hop(0, z + outer - 1 - t)

        @pl.when(t >= outer - 1 - z)
        def _():
            up_hop(1, t - (outer - 1 - z))

        lo = first + (t * (tiles - first)) // (outer - 1)
        hi = first + ((t + 1) * (tiles - first)) // (outer - 1)
        lax.fori_loop(lo, hi, grad_tile, 0)
        return carry

    for t in range(outer - 1):
        line_step(t, 0)
        if t + 2 < outer:
            send_chunk(order[t + 2])

    merged(z)
    umerged(z)

    @pl.when(z > 0)
    def _():
        take(0, z, False)
        take(0, z, True)

    @pl.when(z < outer - 1)
    def _():
        take(1, z, False)
        take(1, z, True)

    for a in range(tenants):
        gdn_ref[a] = acc[a * rank : (a + 1) * rank, :]
        gup_ref[a] = uacc[:, a * oc : (a + 1) * oc]

    for k in range(1, INNER):
        id_copy(k, mi).wait_send()

    def drain(zc, carry):
        for k in range(1, INNER):
            m_copy(zc, k, mi).wait_send()
            u_copy(zc, k, mi).wait_send()

        @pl.when(zc > z)
        def _():
            line_copy(0, zc, False).wait_send()
            line_copy(0, zc, True).wait_send()

        @pl.when(zc < z)
        def _():
            line_copy(1, zc, False).wait_send()
            line_copy(1, zc, True).wait_send()

        return carry

    lax.fori_loop(0, outer, drain, 0)


def per_device(
    features, upstream, frozen_value, adapter_down, adapter_up, block_adapter, block_count, *, n
):
    tokens, width = features.shape
    outs = upstream.shape[1]
    tenants, rank = adapter_down.shape[:2]
    nblk = block_count.shape[0]
    rows = tokens // nblk
    outer = n // INNER
    w, oc = width // n, outs // n
    br = nblk * rank
    lanes = max(br, nblk * oc)
    ar = tenants * rank
    dims = (nblk, rows, rank, tenants, outer, w, oc)
    V = pltpu.VMEM
    D = pltpu.SemaphoreType.DMA
    anyspec = pl.BlockSpec(memory_space=pl.ANY)
    smem = pl.BlockSpec(memory_space=pltpu.SMEM)
    vmem = pl.BlockSpec(memory_space=pltpu.VMEM)
    gin, gdn, gup = pl.pallas_call(
        functools.partial(kernel, dims),
        out_shape=(
            pltpu.VMEM((tokens, width), BF),
            jax.ShapeDtypeStruct((tenants, rank, w), F32),
            jax.ShapeDtypeStruct((tenants, rank, oc), F32),
        ),
        in_specs=[smem, smem] + [anyspec] * 5,
        out_specs=(vmem, vmem, vmem),
        scratch_shapes=[
            V((tokens, width), BF),
            V((tokens, outs), BF),
            V((width, outs), BF),
            V((ar, width), BF),
            V((ar, outs), BF),
            V((br, width), BF),
            V((tokens, outs), BF),
            V((tokens, br), BF),
            V((16, lanes), BF),
            V((INNER, 16, lanes), BF),
            V((outer, INNER, br, w), BF),
            V((outer, INNER, br, w), BF),
            V((outer, INNER, rank, nblk * oc), BF),
            V((outer, INNER, rank, nblk * oc), BF),
            V((ar, INNER * br), BF),
            V((INNER, tenants * oc, nblk * oc), BF),
            V((ar, w), F32),
            V((rank, tenants * oc), F32),
            V((2, outer, ar, w), BF),
            V((2, outer, ar, w), BF),
            V((2, outer, rank, tenants * oc), BF),
            V((2, outer, rank, tenants * oc), BF),
            D((4,)),
            D((outer,)),
            D((INNER,)),
            D((INNER,)),
            D((outer, INNER)),
            D((outer, INNER)),
            D((outer, INNER)),
            D((outer, INNER)),
            D((2, outer)),
            D((2, outer)),
            D((2, outer)),
            D((2, outer)),
        ],
        compiler_params=pltpu.CompilerParams(
            collective_id=0, has_side_effects=True, vmem_limit_bytes=58 * 1024 * 1024
        ),
        cost_estimate=pl.CostEstimate(
            flops=2 * tokens * width * (outs + 3 * br),
            bytes_accessed=2 * (2 * tokens * width + width * outs + ar * width),
            transcendentals=0,
        ),
    )(
        block_adapter.reshape(nblk),
        block_count,
        features,
        upstream,
        frozen_value,
        adapter_down.reshape(ar, width),
        adapter_up.reshape(ar, outs),
    )
    return gin, gdn, gup


def solution(mesh):
    return jax.shard_map(
        functools.partial(per_device, n=mesh.shape["dp"]),
        mesh=mesh,
        in_specs=(
            P(("groups", "dp"), None),
            P(("groups", "dp"), None),
            P(),
            P("groups", None, None),
            P("groups", None, None),
            P(("groups", "dp"), None),
            P(("groups", "dp")),
        ),
        out_specs=(P(("groups", "dp"), None), P("groups", None, "dp"), P("groups", None, "dp")),
        check_vma=False,
    )
```
